32 devices in a mesh: tm: 8 (over y, x, core), col: 4 (over z).
Axes of the slice: x: 2, y: 2, z: 4, core: 2. Of those that a mesh axis runs over, the one named last changes fastest.
Arguments:
- readings: bfloat16 [64, 64, 512], P('tm', 'col'), may hold values from -6 to 6
- block_owner: int32 [64, 1], P('tm'), may hold values from 0 to 7; in each aligned block of 8 rows (0 to 7, 8 to 15, ...) at most 4 rows name the same one
- block_offset: int32 [64], P('tm'), may hold values from 0 to 7
- initial_mean: float32 [64, 512], P('col'), may hold values from -6 to 6
- transition: float32 [512, 512], replicated, may hold values from -1 to 1
- shrink_rate: float32 [512], replicated, may hold values from 0.003125 to 0.078125
- input_map: float32 [512, 512], replicated, may hold values from -0.0625 to 0.0625
- smoother_gain: float32 [512, 512], replicated, may hold values from -1 to 1
Outputs:
- filtered: float32 [64, 64, 512], P('tm', 'col')
- smoothed: float32 [64, 64, 512], P('tm', 'col')
The draws below stay inside these ranges and needn't reach their ends.
Inputs may be any that keep to these rules, and one draw needn't show every extreme that they name: `block_owner`: the blocks of one index of tm name one owner at most 4 times, and in every draw some owner exactly 4 times.
All inputs are finite; a program needn't handle non-finite values.
Results may differ from the reference program's by a relative error of at most 0.0003.
Values may be sent and summed in bfloat16 or wider, within the bound.
A program may use at most 128 MiB of HBM per device.

```python
import math
import jax
import jax.numpy as jnp
import numpy as np
from jax import lax

S = 512
STEPS_DEV = 8
SLOTS = 4
TSTEPS = 64
BATCH = 64
NBLOCKS = 64
N_TM = 8


def shared_rotation(key):
    gaussian = jax.random.normal(jax.random.fold_in(key, 7), (S, S), jnp.float32)
    rotation_basis, triangle = jnp.linalg.qr(gaussian)
    sign_flip = jnp.where(jnp.diagonal(triangle) < 0.0, -1.0, 1.0).astype(jnp.float32)
    return rotation_basis * sign_flip[None, :]


def keeping_rates(key, fastest):
    slowest = 0.25 / TSTEPS
    rates = jnp.exp(jax.random.uniform(key, (S,), jnp.float32, math.log(slowest), math.log(fastest)))
    return jnp.exp(-rates)


def draw_transition(key, part):
    fastest = 8.0 / TSTEPS
    rotation = shared_rotation(key)
    keeping = keeping_rates(jax.random.fold_in(key, 11), fastest)
    return rotation * keeping[None, :]


def draw_smoother_gain(key, part):
    fastest = 8.0 / TSTEPS
    rotation = shared_rotation(key)
    keeping = keeping_rates(jax.random.fold_in(key, 23), fastest)
    return keeping[:, None] * jnp.transpose(rotation)


def place_ends(entries, key, smallest, high):
    longest = entries.shape.index(max(entries.shape))
    spots = []
    for shift in (0, 1):
        where = [jax.random.randint(jax.random.fold_in(key, axis), (), 0, length) for axis, length in enumerate(entries.shape)]
        where[longest] = (where[longest] + shift) % entries.shape[longest]
        spots.append(tuple(where))
    return entries.at[spots[0]].set(smallest).at[spots[1]].set(high)


def block_levels(key, extent, shards, low, high):
    def one(position, shards_of):
        steps = jax.random.uniform(jax.random.fold_in(jax.random.fold_in(key, 6), position), (shards_of,), jnp.float32, low / len(shards), high / len(shards))
        return jnp.repeat(jnp.exp(steps), extent[position] // shards_of).reshape((-1,) + (1,) * (len(extent) - position - 1))

    gain = one(*shards[0])
    for cut in shards[1:]:
        gain = gain * one(*cut)
    return gain


def deal_out(rng, own, number, rows, amount, top, limit, lean):
    sequence = jax.random.permutation(rng, amount)
    packed, usual = shares(amount, rows * top, limit, lean, True), shares(amount, rows * top, limit, lean, False)
    places = jnp.arange(amount)

    def named(sizes, turn):
        used = int((sizes > 0).sum())
        fixed = max(1, used // 4)
        passed = fixed + (places - fixed + turn * (used - fixed)) % max(1, amount - fixed)
        return jnp.zeros((amount,), jnp.int32).at[sequence[jnp.where(places < fixed, places, passed)]].set(jnp.asarray(sizes, jnp.int32))

    sizes = jnp.where(number % 4 == 0, named(packed, number // 4), named(usual, number - number // 4 - 1))
    mixed = jax.random.permutation(jax.random.fold_in(own, 3), amount)
    giver, receiver = mixed[0:amount // 2 * 2:2], mixed[1:amount // 2 * 2:2]
    margin = jnp.minimum(sizes[giver] - 1, limit - sizes[receiver]) // 2
    margin = jnp.where((giver == sequence[0]) | (receiver == sequence[0]) | (sizes[receiver] == 0), 0, jnp.maximum(margin, 0))
    passed = jax.random.randint(jax.random.fold_in(own, 4), (amount // 2,), 0, 1 << 20) % (margin + 1)
    sizes = sizes.at[giver].add(-passed).at[receiver].add(passed)
    members = jnp.searchsorted(jnp.cumsum(sizes), jnp.arange(rows * top), side="right").astype(jnp.int32)
    grid = members.reshape(top, rows).T
    grid = grid[jax.random.permutation(jax.random.fold_in(own, 1), rows)]
    turn = jax.random.randint(jax.random.fold_in(own, 2), (rows, 1), 0, top)
    return jnp.take_along_axis(grid, (jnp.arange(top)[None, :] + turn) % top, axis=1)


def shares(amount, total, most, slope, full):
    loads = [(1 << 20) // math.isqrt(grade ** slope) + 1 for grade in range(1, amount + 1)]
    largest = most if full else min(most, max(-(-total // amount), total * loads[0] // sum(loads)))
    least = 1 if total - largest >= amount - 1 else 0
    given, spare = [largest] + [least] * (amount - 1), total - largest - least * (amount - 1)
    while spare > 0:
        movable = [i for i in range(1, amount) if given[i] < largest] or [i for i in range(1, amount) if given[i] < most]
        mass, left = sum([loads[i] for i in movable]), spare
        for i in movable:
            more = min(most - given[i], max(1, left * loads[i] // mass), spare)
            given[i] = given[i] + more
            spare = spare - more
    return np.array(given)


def scatter_about(own_key, extent, deviation, limit, split=(), kind=jnp.bfloat16):
    factor_of = block_levels(own_key, extent, split, -0.22, 0.18) if split else 1.0
    values = jax.random.normal(own_key, extent, jnp.float32) * deviation * factor_of
    return jnp.minimum(jnp.maximum(values, -limit), limit).astype(kind)


def setup_inputs(seed: int = 0) -> dict:
    splits = jax.random.split(jax.random.key(seed), 9)
    readings = scatter_about(splits[0], (NBLOCKS, BATCH, S), 1.0, 6.0, ((0, 8), (1, 4)))
    block_owner_keys = jax.random.split(jax.random.fold_in(splits[1], 1), NBLOCKS // STEPS_DEV)
    block_owner_turns = jax.random.permutation(jax.random.fold_in(splits[1], 3), NBLOCKS // STEPS_DEV)
    block_owner = jax.vmap(lambda own, number: deal_out(jax.random.fold_in(splits[1], 2), own, number, STEPS_DEV, N_TM, 1, SLOTS, 2))(block_owner_keys, block_owner_turns).reshape((NBLOCKS, 1))
    block_offset = place_ends(jax.random.randint(splits[2], (NBLOCKS,), 0, STEPS_DEV), jax.random.fold_in(splits[2], 1), 0, STEPS_DEV - 1).astype(jnp.int32)
    initial_mean = scatter_about(splits[3], (BATCH, S), 1.0, 6.0, ((0, 4),), jnp.float32)
    transition = draw_transition(jax.random.fold_in(splits[8], 71), 0)
    shrink_rate = jnp.clip(jnp.exp(jax.random.uniform(splits[5], (S,), jnp.float32, math.log(0.003125), math.log(0.078125))), 0.003125, 0.078125)
    input_map = scatter_about(splits[6], (S, S), (S * 16) ** -0.5, 0.0625, (), jnp.float32)
    smoother_gain = draw_smoother_gain(jax.random.fold_in(splits[8], 71), 0)
    return {"readings": readings, "block_owner": block_owner, "block_offset": block_offset, "initial_mean": initial_mean, "transition": transition, "shrink_rate": shrink_rate, "input_map": input_map, "smoother_gain": smoother_gain}


PRECISE = lax.Precision.HIGHEST

def matmul(left, right):
    return jnp.dot(left.astype(jnp.float32), right.astype(jnp.float32), precision=PRECISE, preferred_element_type=jnp.float32)

def reference(readings, block_owner, block_offset, initial_mean, transition, shrink_rate, input_map, smoother_gain):
    step_index = (block_owner[:, 0] * STEPS_DEV + block_offset).astype(jnp.int32)
    inflow = jax.ops.segment_sum(readings.astype(jnp.float32), step_index, num_segments=TSTEPS)
    counts = jax.ops.segment_sum(jnp.ones(step_index.shape, jnp.float32), step_index, num_segments=TSTEPS)
    drive = matmul(inflow.reshape(TSTEPS * BATCH, S), input_map).reshape(TSTEPS, BATCH, S)
    factor = jnp.exp(-counts[:, None] * shrink_rate[None, :])

    def forward(mean_now, inputs):
        push, scaling = inputs
        mean_now = matmul(mean_now, transition) * scaling[None, :] + push
        return (mean_now, mean_now)
    final_mean, filtered = lax.scan(forward, initial_mean, (drive, factor))
    identity = jnp.eye(S, dtype=jnp.float32)
    blend = identity - matmul(transition, smoother_gain)
    mixed = matmul(filtered.reshape(TSTEPS * BATCH, S), blend).reshape(TSTEPS, BATCH, S)

    def backward(state_now, inputs):
        state_now = matmul(state_now, smoother_gain) + inputs
        return (state_now, state_now)
    closing = filtered[TSTEPS - 1]
    state_end, earlier = lax.scan(backward, closing, mixed[:TSTEPS - 1], reverse=True)
    smoothed = jnp.concatenate([earlier, closing[None]], axis=0)
    return (filtered, smoothed)
```

```python
import functools
import jax
import jax.numpy as jnp
from jax import lax
from jax.experimental import pallas as pl
from jax.experimental.pallas import tpu as pltpu
from jax.sharding import PartitionSpec as P

STEPS_DEV = 8
BF = jnp.bfloat16
F32 = jnp.float32


def halves(x):
    hi = x.astype(BF)
    return hi, (x - hi.astype(F32)).astype(BF)


def dot(a, b):
    return jnp.dot(a, b, preferred_element_type=F32)


def product(x, hi_ref, lo_ref):
    rows = x.shape[0]
    hi, lo = halves(x)
    both = dot(jnp.concatenate([hi, lo], axis=0), hi_ref[...])
    return both[:rows] + both[rows:] + dot(hi, lo_ref[...])


def split_into(x, hi_ref, lo_ref):
    hi, lo = halves(x)
    hi_ref[...] = hi
    lo_ref[...] = lo


def square_into(x_ref, y_hi, y_lo, out):
    width = x_ref.shape[0]
    chunk = 128

    @pl.loop(0, width // chunk)
    def _(i):
        rows = pl.ds(pl.multiple_of(i * chunk, chunk), chunk)
        out(rows, product(x_ref[rows, :], y_hi, y_lo))


def kernel(
    slabs, levels, readings, target, initial, transition, shrink, input_map, gain,
    filtered, smoothed,
    a_hi, a_lo, w_hi, w_lo, b_hi, b_lo, g_hi, g_lo, square,
    drive, factor, means, mixed, pairs, quads, sums,
):
    me = lax.axis_index("tm")
    width = transition.shape[0]
    batch = initial.shape[0]
    steps = slabs * STEPS_DEV
    per = STEPS_DEV * batch
    split_into(transition[...], a_hi, a_lo)
    split_into(input_map[...], w_hi, w_lo)
    split_into(gain[...], g_hi.at[0], g_lo.at[0])

    def put_blend(rows, value):
        row = lax.broadcasted_iota(jnp.int32, value.shape, 0) + rows.start
        col = lax.broadcasted_iota(jnp.int32, value.shape, 1)
        blend = jnp.where(row == col, 1.0, 0.0) - value
        split_into(blend, b_hi.at[rows, :], b_lo.at[rows, :])

    square_into(transition, g_hi.at[0], g_lo.at[0], put_blend)

    for level in range(1, levels):
        def put_power(rows, value):
            square[level % 2, rows, :] = value
            split_into(value, g_hi.at[level, rows, :], g_lo.at[level, rows, :])

        source = gain if level == 1 else square.at[(level - 1) % 2]
        square_into(source, g_hi.at[level - 1], g_lo.at[level - 1], put_power)

    count = jnp.zeros((steps, 1), F32)
    for slab in range(slabs):
        hit = lax.broadcasted_iota(jnp.int32, (steps, per), 0) * batch == target[pl.ds(slab, 1), :]
        count += jnp.sum(jnp.where(hit, 1.0, 0.0), axis=1, keepdims=True)
    factor[...] = jnp.exp(-count * shrink[...])

    @pl.loop(0, slabs)
    def _(to):
        inflow = jnp.zeros((per, width), F32)
        row = lax.broadcasted_iota(jnp.int32, (per, per), 0) + to * per
        for slab in range(slabs):
            pick = jnp.where(row == target[pl.ds(slab, 1), :], 1.0, 0.0).astype(BF)
            inflow += dot(pick, readings[pl.ds(slab * per, per), :])
        pushes = product(inflow, w_hi, w_lo)
        drive[pl.ds(to * STEPS_DEV, STEPS_DEV)] = pushes.reshape(STEPS_DEV, batch, width)

    def forward(step, mean):
        mean = product(mean, a_hi, a_lo) * factor[pl.ds(step, 1), :] + drive[step]
        means[step] = mean
        return mean

    lax.fori_loop(0, steps, forward, initial[...], unroll=4)
    filtered[...] = means[pl.ds(me * STEPS_DEV, STEPS_DEV)]

    @pl.loop(0, slabs)
    def _(slab):
        part = pl.ds(slab * STEPS_DEV, STEPS_DEV)
        mix = product(means[part].reshape(per, width), b_hi, b_lo)
        mixed[part] = mix.reshape(STEPS_DEV, batch, width)

    mixed[steps - 1] = means[steps - 1]

    def fold(values, level):
        number = values.shape[0] // 2
        values = values.reshape(number, 2, batch, width)
        odd = values[:, 1].reshape(number * batch, width)
        moved = product(odd, g_hi.at[level], g_lo.at[level])
        return values[:, 0] + moved.reshape(number, batch, width)

    @pl.loop(0, slabs // 2)
    def _(i):
        part = pl.ds(i * 2 * STEPS_DEV, 2 * STEPS_DEV)
        pairs[pl.ds(i * STEPS_DEV, STEPS_DEV)] = fold(mixed[part], 0)

    quads[...] = fold(pairs[...], 1)
    sums[pl.ds(0, slabs)] = fold(quads[...], 2)
    sums[pl.ds(slabs, slabs)] = jnp.zeros((slabs, batch, width), F32)
    later = sums[pl.ds(me + 1, slabs)]
    for level in range(3, levels):
        later = fold(later, level)
    carry = later[0]

    def back(state, level):
        return product(state, g_hi.at[level], g_lo.at[level])

    at0 = sums[me] + back(carry, 3)
    at4 = quads[me * 2 + 1] + back(carry, 2)
    two = back(jnp.concatenate([at4, carry], axis=0), 1)
    at2 = pairs[me * 4 + 1] + two[:batch]
    at6 = pairs[me * 4 + 3] + two[batch:]
    one = back(jnp.concatenate([at2, at4, at6, carry], axis=0), 0)
    base = me * STEPS_DEV
    smoothed[0] = at0
    smoothed[2] = at2
    smoothed[4] = at4
    smoothed[6] = at6
    for i in range(4):
        smoothed[2 * i + 1] = mixed[base + 2 * i + 1] + one[i * batch:(i + 1) * batch]


def per_device(
    readings, block_owner, block_offset, initial_mean, transition, shrink_rate, input_map, smoother_gain
):
    slabs = lax.axis_size("tm")
    blocks, batch, width = readings.shape
    steps = slabs * STEPS_DEV
    levels = 3 + (slabs - 1).bit_length()
    step = block_owner[:, 0] * STEPS_DEV + block_offset
    target = (step[:, None] * batch + jnp.arange(batch, dtype=jnp.int32)[None, :]).reshape(1, -1)
    readings = lax.all_gather(readings.reshape(-1, width), "tm", axis=0, tiled=True)
    target = lax.all_gather(target, "tm", axis=0, tiled=True)
    out = jax.ShapeDtypeStruct((STEPS_DEV, batch, width), F32)
    return pl.pallas_call(
        functools.partial(kernel, slabs, levels),
        out_shape=(out, out),
        in_specs=[pl.BlockSpec(memory_space=pltpu.VMEM)] * 7,
        out_specs=[pl.BlockSpec(memory_space=pltpu.VMEM)] * 2,
        scratch_shapes=[pltpu.VMEM((width, width), BF)] * 6
        + [pltpu.VMEM((levels, width, width), BF)] * 2
        + [
            pltpu.VMEM((2, width, width), F32),
            pltpu.VMEM((steps, batch, width), F32),
            pltpu.VMEM((steps, width), F32),
            pltpu.VMEM((steps, batch, width), F32),
            pltpu.VMEM((steps, batch, width), F32),
            pltpu.VMEM((steps // 2, batch, width), F32),
            pltpu.VMEM((steps // 4, batch, width), F32),
            pltpu.VMEM((2 * slabs, batch, width), F32),
        ],
        compiler_params=pltpu.CompilerParams(vmem_limit_bytes=56 * 2**20),
    )(readings, target, initial_mean, transition, shrink_rate.reshape(1, -1), input_map, smoother_gain)


def solution(mesh):
    in_specs = (P("tm", "col", None), P("tm", None), P("tm"), P("col", None), P(), P(), P(), P())
    out_specs = (P("tm", "col", None), P("tm", "col", None))
    return jax.shard_map(
        per_device, mesh=mesh, in_specs=in_specs, out_specs=out_specs, check_vma=False
    )
```

```python
import functools
import jax
import jax.numpy as jnp
from jax import lax
from jax.experimental import pallas as pl
from jax.experimental.pallas import tpu as pltpu
from jax.sharding import PartitionSpec as P

STEPS_DEV = 8
BF = jnp.bfloat16
F32 = jnp.float32
MESH = pl.DeviceIdType.MESH


def halves(x):
    hi = x.astype(BF)
    return hi, (x - hi.astype(F32)).astype(BF)


def dot(a, b):
    return jnp.dot(a, b, preferred_element_type=F32)


def product(x, hi_ref, lo_ref):
    rows = x.shape[0]
    hi, lo = halves(x)
    both = dot(jnp.concatenate([hi, lo], axis=0), hi_ref[...])
    return both[:rows] + both[rows:] + dot(hi, lo_ref[...])


def split_into(x, hi_ref, lo_ref):
    hi, lo = halves(x)
    hi_ref[...] = hi
    lo_ref[...] = lo


def square_into(x_ref, y_hi, y_lo, out):
    width = x_ref.shape[0]
    chunk = 128

    @pl.loop(0, width // chunk)
    def _(i):
        rows = pl.ds(pl.multiple_of(i * chunk, chunk), chunk)
        out(rows, product(x_ref[rows, :], y_hi, y_lo))


def kernel(
    slabs, levels, readings, owner, offset, initial, shrink, transition_in, input_map_in, gain_in,
    filtered, smoothed,
    arrived, target, transition, input_map, gain,
    a_hi, a_lo, w_hi, w_lo, b_hi, b_lo, g_hi, g_lo, square,
    drive, factor, means, mixed, pairs, quads, sums,
    load_sem, own_sem, send_sem, recv_sem, send_target_sem, recv_target_sem,
):
    me = lax.axis_index("tm")
    width = transition.shape[0]
    batch = initial.shape[0]
    steps = slabs * STEPS_DEV
    per = STEPS_DEV * batch

    barrier = pltpu.get_barrier_semaphore()
    for hop in range(1, slabs):
        pl.semaphore_signal(
            barrier, inc=1, device_id={"tm": lax.rem(me + hop, slabs)}, device_id_type=MESH
        )
    loads = [
        pltpu.make_async_copy(source, into, load_sem.at[i])
        for i, (source, into) in enumerate(
            ((gain_in, gain), (transition_in, transition), (input_map_in, input_map))
        )
    ]
    for load in loads:
        load.start()
    mine = pl.ds(me * STEPS_DEV, STEPS_DEV)
    own = pltpu.make_async_copy(readings, arrived.at[mine], own_sem)
    own.start()

    blocks = owner.shape[1]
    square_shape = (blocks, blocks)
    diagonal = lax.broadcasted_iota(jnp.int32, square_shape, 0) == lax.broadcasted_iota(
        jnp.int32, square_shape, 1
    )
    step = (owner[...] * STEPS_DEV + offset[...]).astype(F32)
    step = jnp.sum(jnp.where(diagonal, step, 0.0), axis=1, keepdims=True)
    lane = lax.broadcasted_iota(jnp.int32, (blocks, per), 1)
    block = lax.broadcasted_iota(jnp.int32, (blocks, per), 0)
    inside = lane - block * batch
    here = jnp.logical_and(inside >= 0, inside < batch)
    row = step * batch + inside.astype(F32)
    target[me] = jnp.sum(jnp.where(here, row, 0.0), axis=0, keepdims=True)

    pl.semaphore_wait(barrier, slabs - 1)
    copies = []
    for hop in range(1, slabs):
        peer = {"tm": lax.rem(me + hop, slabs)}
        copies.append(
            pltpu.make_async_remote_copy(
                readings, arrived.at[mine], send_sem.at[hop], recv_sem.at[hop],
                device_id=peer, device_id_type=MESH,
            )
        )
        copies.append(
            pltpu.make_async_remote_copy(
                target.at[me], target.at[me], send_target_sem.at[hop], recv_target_sem.at[hop],
                device_id=peer, device_id_type=MESH,
            )
        )
    for copy in copies:
        copy.start()

    loads[0].wait()
    split_into(gain[...], g_hi.at[0], g_lo.at[0])
    loads[1].wait()
    split_into(transition[...], a_hi, a_lo)
    loads[2].wait()
    split_into(input_map[...], w_hi, w_lo)

    def put_blend(rows, value):
        row = lax.broadcasted_iota(jnp.int32, value.shape, 0) + rows.start
        col = lax.broadcasted_iota(jnp.int32, value.shape, 1)
        blend = jnp.where(row == col, 1.0, 0.0) - value
        split_into(blend, b_hi.at[rows, :], b_lo.at[rows, :])

    square_into(transition, g_hi.at[0], g_lo.at[0], put_blend)

    for level in range(1, levels):
        def put_power(rows, value):
            square[level % 2, rows, :] = value
            split_into(value, g_hi.at[level, rows, :], g_lo.at[level, rows, :])

        source = gain if level == 1 else square.at[(level - 1) % 2]
        square_into(source, g_hi.at[level - 1], g_lo.at[level - 1], put_power)

    own.wait()
    for copy in copies:
        copy.wait_recv()

    count = jnp.zeros((steps, 1), F32)
    for slab in range(slabs):
        hit = lax.broadcasted_iota(jnp.int32, (steps, per), 0)
        behind = target[slab] - hit.astype(F32) * batch
        hit = jnp.logical_and(behind >= 0.0, behind < batch)
        count += jnp.sum(jnp.where(hit, 1.0, 0.0), axis=1, keepdims=True)
    count = count / batch
    factor[...] = jnp.exp(-count * shrink[...])

    @pl.loop(0, slabs)
    def _(to):
        inflow = jnp.zeros((per, width), F32)
        row = (lax.broadcasted_iota(jnp.int32, (per, per), 0) + to * per).astype(F32)
        for slab in range(slabs):
            pick = jnp.where(row == target[slab], 1.0, 0.0).astype(BF)
            inflow += dot(pick, arrived[pl.ds(slab * STEPS_DEV, STEPS_DEV)].reshape(per, width))
        pushes = product(inflow, w_hi, w_lo)
        drive[pl.ds(to * STEPS_DEV, STEPS_DEV)] = pushes.reshape(STEPS_DEV, batch, width)

    def forward(step, mean):
        mean = product(mean, a_hi, a_lo) * factor[pl.ds(step, 1), :] + drive[step]
        means[step] = mean
        return mean

    lax.fori_loop(0, steps, forward, initial[...], unroll=4)
    filtered[...] = means[pl.ds(me * STEPS_DEV, STEPS_DEV)]

    @pl.loop(0, slabs)
    def _(slab):
        part = pl.ds(slab * STEPS_DEV, STEPS_DEV)
        mix = product(means[part].reshape(per, width), b_hi, b_lo)
        mixed[part] = mix.reshape(STEPS_DEV, batch, width)

    mixed[steps - 1] = means[steps - 1]

    def fold(values, level):
        number = values.shape[0] // 2
        values = values.reshape(number, 2, batch, width)
        odd = values[:, 1].reshape(number * batch, width)
        moved = product(odd, g_hi.at[level], g_lo.at[level])
        return values[:, 0] + moved.reshape(number, batch, width)

    @pl.loop(0, slabs // 2)
    def _(i):
        part = pl.ds(i * 2 * STEPS_DEV, 2 * STEPS_DEV)
        pairs[pl.ds(i * STEPS_DEV, STEPS_DEV)] = fold(mixed[part], 0)

    quads[...] = fold(pairs[...], 1)
    sums[pl.ds(0, slabs)] = fold(quads[...], 2)
    sums[pl.ds(slabs, slabs)] = jnp.zeros((slabs, batch, width), F32)
    later = sums[pl.ds(me + 1, slabs)]
    for level in range(3, levels):
        later = fold(later, level)
    carry = later[0]

    def back(state, level):
        return product(state, g_hi.at[level], g_lo.at[level])

    at0 = sums[me] + back(carry, 3)
    at4 = quads[me * 2 + 1] + back(carry, 2)
    two = back(jnp.concatenate([at4, carry], axis=0), 1)
    at2 = pairs[me * 4 + 1] + two[:batch]
    at6 = pairs[me * 4 + 3] + two[batch:]
    one = back(jnp.concatenate([at2, at4, at6, carry], axis=0), 0)
    base = me * STEPS_DEV
    smoothed[0] = at0
    smoothed[2] = at2
    smoothed[4] = at4
    smoothed[6] = at6
    for i in range(4):
        smoothed[2 * i + 1] = mixed[base + 2 * i + 1] + one[i * batch:(i + 1) * batch]

    for copy in copies:
        copy.wait_send()


def per_device(
    readings, block_owner, block_offset, initial_mean, transition, shrink_rate, input_map, smoother_gain
):
    slabs = lax.axis_size("tm")
    blocks, batch, width = readings.shape
    steps = slabs * STEPS_DEV
    per = STEPS_DEV * batch
    levels = 3 + (slabs - 1).bit_length()
    out = jax.ShapeDtypeStruct((STEPS_DEV, batch, width), F32)
    return pl.pallas_call(
        functools.partial(kernel, slabs, levels),
        out_shape=(out, out),
        in_specs=[pl.BlockSpec(memory_space=pl.ANY)]
        + [pl.BlockSpec(memory_space=pltpu.VMEM)] * 4
        + [pl.BlockSpec(memory_space=pl.ANY)] * 3,
        out_specs=[pl.BlockSpec(memory_space=pltpu.VMEM)] * 2,
        scratch_shapes=[
            pltpu.VMEM((slabs * blocks, batch, width), BF),
            pltpu.VMEM((slabs, 1, per), F32),
        ]
        + [pltpu.VMEM((width, width), F32)] * 3
        + [pltpu.VMEM((width, width), BF)] * 6
        + [pltpu.VMEM((levels, width, width), BF)] * 2
        + [
            pltpu.VMEM((2, width, width), F32),
            pltpu.VMEM((steps, batch, width), F32),
            pltpu.VMEM((steps, width), F32),
            pltpu.VMEM((steps, batch, width), F32),
            pltpu.VMEM((steps, batch, width), F32),
            pltpu.VMEM((steps // 2, batch, width), F32),
            pltpu.VMEM((steps // 4, batch, width), F32),
            pltpu.VMEM((2 * slabs, batch, width), F32),
            pltpu.SemaphoreType.DMA((3,)),
            pltpu.SemaphoreType.DMA,
        ]
        + [pltpu.SemaphoreType.DMA((slabs,))] * 4,
        compiler_params=pltpu.CompilerParams(
            vmem_limit_bytes=56 * 2**20, collective_id=0, has_side_effects=True
        ),
    )(
        readings, block_owner.reshape(1, -1), block_offset.reshape(1, -1), initial_mean,
        shrink_rate.reshape(1, -1), transition, input_map, smoother_gain,
    )


def solution(mesh):
    in_specs = (P("tm", "col", None), P("tm", None), P("tm"), P("col", None), P(), P(), P(), P())
    out_specs = (P("tm", "col", None), P("tm", "col", None))
    return jax.shard_map(
        per_device, mesh=mesh, in_specs=in_specs, out_specs=out_specs, check_vma=False
    )
```

```python
import functools
import jax
import jax.numpy as jnp
from jax import lax
from jax.experimental import pallas as pl
from jax.experimental.pallas import tpu as pltpu
from jax.sharding import PartitionSpec as P

STEPS_DEV = 8
BF = jnp.bfloat16
F32 = jnp.float32
MESH = pl.DeviceIdType.MESH


def halves(x):
    hi = x.astype(BF)
    return hi, (x - hi.astype(F32)).astype(BF)


def dot(a, b):
    return jnp.dot(a, b, preferred_element_type=F32)


def product(x, hi_ref, lo_ref):
    rows = x.shape[0]
    hi, lo = halves(x)
    both = dot(jnp.concatenate([hi, lo], axis=0), hi_ref[...])
    return both[:rows] + both[rows:] + dot(hi, lo_ref[...])


def split_into(x, hi_ref, lo_ref):
    hi, lo = halves(x)
    hi_ref[...] = hi
    lo_ref[...] = lo


def square_into(x_ref, y_hi, y_lo, out):
    width = x_ref.shape[0]
    chunk = 128

    @pl.loop(0, width // chunk)
    def _(i):
        rows = pl.ds(pl.multiple_of(i * chunk, chunk), chunk)
        out(rows, product(x_ref[rows, :], y_hi, y_lo))


def kernel(
    slabs, levels, readings, owner, offset, initial, shrink, transition_in, input_map_in, gain_in,
    filtered, smoothed,
    arrived, target, transition, input_map, gain,
    a_hi, a_lo, w_hi, w_lo, b_hi, b_lo, g_hi, g_lo, square,
    inflow, drive, factor, means, mixed, pairs, quads, sums,
    load_sem, own_sem, send_sem, recv_sem, send_target_sem, recv_target_sem,
):
    me = lax.axis_index("tm")
    width = transition.shape[0]
    batch = initial.shape[0]
    steps = slabs * STEPS_DEV
    per = STEPS_DEV * batch

    barrier = pltpu.get_barrier_semaphore()
    for hop in range(1, slabs):
        pl.semaphore_signal(
            barrier, inc=1, device_id={"tm": lax.rem(me + hop, slabs)}, device_id_type=MESH
        )
    loads = [
        pltpu.make_async_copy(source, into, load_sem.at[i])
        for i, (source, into) in enumerate(
            ((gain_in, gain), (transition_in, transition), (input_map_in, input_map))
        )
    ]
    for load in loads:
        load.start()
    mine = pl.ds(me * STEPS_DEV, STEPS_DEV)
    own = pltpu.make_async_copy(readings, arrived.at[mine], own_sem)
    own.start()

    blocks = owner.shape[1]
    square_shape = (blocks, blocks)
    diagonal = lax.broadcasted_iota(jnp.int32, square_shape, 0) == lax.broadcasted_iota(
        jnp.int32, square_shape, 1
    )
    step = (owner[...] * STEPS_DEV + offset[...]).astype(F32)
    step = jnp.sum(jnp.where(diagonal, step, 0.0), axis=1, keepdims=True)
    lane = lax.broadcasted_iota(jnp.int32, (blocks, per), 1)
    block = lax.broadcasted_iota(jnp.int32, (blocks, per), 0)
    inside = lane - block * batch
    here = jnp.logical_and(inside >= 0, inside < batch)
    row = step * batch + inside.astype(F32)
    target[me] = jnp.sum(jnp.where(here, row, 0.0), axis=0, keepdims=True)

    pl.semaphore_wait(barrier, slabs - 1)
    duos = slabs // 2
    duo, side = lax.div(me, 2), lax.rem(me, 2)
    sibling = {"tm": duo * 2 + 1 - side}

    def block_of(hop):
        source = lax.rem(duo + duos - hop, duos) * 2 + side
        return arrived.at[pl.ds(source * STEPS_DEV, STEPS_DEV)]

    directs, forwards, labels = [], [None], []
    for hop in range(duos):
        peer = sibling if hop == 0 else {"tm": lax.rem(duo + hop, duos) * 2 + side}
        directs.append(
            pltpu.make_async_remote_copy(
                readings, arrived.at[mine], send_sem.at[hop], recv_sem.at[hop],
                device_id=peer, device_id_type=MESH,
            )
        )
    for hop in range(1, duos):
        forwards.append(
            pltpu.make_async_remote_copy(
                block_of(hop), block_of(hop), send_sem.at[duos + hop], recv_sem.at[duos + hop],
                device_id=sibling, device_id_type=MESH,
            )
        )
    for hop in range(1, slabs):
        labels.append(
            pltpu.make_async_remote_copy(
                target.at[me], target.at[me], send_target_sem.at[hop], recv_target_sem.at[hop],
                device_id={"tm": lax.rem(me + hop, slabs)}, device_id_type=MESH,
            )
        )
    for copy in directs[1:] + directs[:1] + labels:
        copy.start()

    def forward_block(hop):
        if hop < duos:
            directs[hop].wait_recv()
            forwards[hop].start()

    loads[0].wait()
    split_into(gain[...], g_hi.at[0], g_lo.at[0])
    loads[1].wait()
    split_into(transition[...], a_hi, a_lo)
    loads[2].wait()
    split_into(input_map[...], w_hi, w_lo)

    def put_blend(rows, value):
        row = lax.broadcasted_iota(jnp.int32, value.shape, 0) + rows.start
        col = lax.broadcasted_iota(jnp.int32, value.shape, 1)
        blend = jnp.where(row == col, 1.0, 0.0) - value
        split_into(blend, b_hi.at[rows, :], b_lo.at[rows, :])

    def put_power(level, rows, value):
        square[level % 2, rows, :] = value
        split_into(value, g_hi.at[level, rows, :], g_lo.at[level, rows, :])

    def power(level):
        source = gain if level == 1 else square.at[(level - 1) % 2]
        square_into(
            source, g_hi.at[level - 1], g_lo.at[level - 1], functools.partial(put_power, level)
        )

    span = min(2 * per, steps * batch)

    def add_duo(hop):
        which = lax.rem(duo + duos - hop, duos) * 2
        rows_of = jnp.concatenate([target[which], target[which + 1]], axis=1)

        @pl.loop(0, steps * batch // span)
        def _(i):
            row = (lax.broadcasted_iota(jnp.int32, (span, 2 * per), 0) + i * span).astype(F32)
            pick = jnp.where(row == rows_of, 1.0, 0.0).astype(BF)
            values = arrived[pl.ds(which * STEPS_DEV, 2 * STEPS_DEV)].reshape(2 * per, width)
            part = pl.ds(pl.multiple_of(i * span, span), span)
            added = dot(pick, values)
            inflow[part, :] = added if hop == 0 else inflow[part, :] + added

    square_into(transition, g_hi.at[0], g_lo.at[0], put_blend)
    forward_block(1)
    power(1)
    forward_block(2)
    own.wait()
    directs[0].wait_recv()
    for label in labels:
        label.wait_recv()
    add_duo(0)
    for hop in range(3, duos):
        forward_block(hop)
    for level in range(2, levels):
        power(level)
    for hop in range(1, duos):
        forwards[hop].wait_recv()
        add_duo(hop)

    count = jnp.zeros((steps, 1), F32)
    for slab in range(slabs):
        hit = lax.broadcasted_iota(jnp.int32, (steps, per), 0)
        behind = target[slab] - hit.astype(F32) * batch
        hit = jnp.logical_and(behind >= 0.0, behind < batch)
        count += jnp.sum(jnp.where(hit, 1.0, 0.0), axis=1, keepdims=True)
    count = count / batch
    factor[...] = jnp.exp(-count * shrink[...])

    def push(slab):
        rows = pl.ds(pl.multiple_of(slab * per, per), per)
        value = product(inflow[rows, :], w_hi, w_lo)
        drive[pl.ds(slab * STEPS_DEV, STEPS_DEV)] = value.reshape(STEPS_DEV, batch, width)

    def mix(slab):
        part = pl.ds(slab * STEPS_DEV, STEPS_DEV)
        value = product(means[part].reshape(per, width), b_hi, b_lo)
        mixed[part] = value.reshape(STEPS_DEV, batch, width)

    def advance(slab, mean):
        for i in range(STEPS_DEV):
            step = slab * STEPS_DEV + i
            mean = product(mean, a_hi, a_lo) * factor[pl.ds(step, 1), :] + drive[step]
            means[step] = mean
        return mean

    push(0)
    push(1)
    mean = advance(0, initial[...])

    def body(slab, mean):
        push(slab + 1)
        mix(slab - 1)
        return advance(slab, mean)

    mean = lax.fori_loop(1, slabs - 1, body, mean)
    mix(slabs - 2)
    advance(slabs - 1, mean)
    mix(slabs - 1)
    filtered[...] = means[mine]
    mixed[steps - 1] = means[steps - 1]

    def fold(values, level):
        number = values.shape[0] // 2
        values = values.reshape(number, 2, batch, width)
        odd = values[:, 1].reshape(number * batch, width)
        moved = product(odd, g_hi.at[level], g_lo.at[level])
        return values[:, 0] + moved.reshape(number, batch, width)

    @pl.loop(0, slabs // 2)
    def _(i):
        part = pl.ds(i * 2 * STEPS_DEV, 2 * STEPS_DEV)
        pairs[pl.ds(i * STEPS_DEV, STEPS_DEV)] = fold(mixed[part], 0)

    quads[...] = fold(pairs[...], 1)
    sums[pl.ds(0, slabs)] = fold(quads[...], 2)
    sums[pl.ds(slabs, slabs)] = jnp.zeros((slabs, batch, width), F32)
    later = sums[pl.ds(me + 1, slabs)]
    for level in range(3, levels):
        later = fold(later, level)
    carry = later[0]

    def back(state, level):
        return product(state, g_hi.at[level], g_lo.at[level])

    at0 = sums[me] + back(carry, 3)
    at4 = quads[me * 2 + 1] + back(carry, 2)
    two = back(jnp.concatenate([at4, carry], axis=0), 1)
    at2 = pairs[me * 4 + 1] + two[:batch]
    at6 = pairs[me * 4 + 3] + two[batch:]
    one = back(jnp.concatenate([at2, at4, at6, carry], axis=0), 0)
    base = me * STEPS_DEV
    smoothed[0] = at0
    smoothed[2] = at2
    smoothed[4] = at4
    smoothed[6] = at6
    for i in range(4):
        smoothed[2 * i + 1] = mixed[base + 2 * i + 1] + one[i * batch:(i + 1) * batch]

    for copy in directs + forwards[1:] + labels:
        copy.wait_send()


def per_device(
    readings, block_owner, block_offset, initial_mean, transition, shrink_rate, input_map, smoother_gain
):
    slabs = lax.axis_size("tm")
    blocks, batch, width = readings.shape
    steps = slabs * STEPS_DEV
    per = STEPS_DEV * batch
    levels = 3 + (slabs - 1).bit_length()
    out = jax.ShapeDtypeStruct((STEPS_DEV, batch, width), F32)
    return pl.pallas_call(
        functools.partial(kernel, slabs, levels),
        out_shape=(out, out),
        in_specs=[pl.BlockSpec(memory_space=pl.ANY)]
        + [pl.BlockSpec(memory_space=pltpu.VMEM)] * 4
        + [pl.BlockSpec(memory_space=pl.ANY)] * 3,
        out_specs=[pl.BlockSpec(memory_space=pltpu.VMEM)] * 2,
        scratch_shapes=[
            pltpu.VMEM((slabs * blocks, batch, width), BF),
            pltpu.VMEM((slabs, 1, per), F32),
        ]
        + [pltpu.VMEM((width, width), F32)] * 3
        + [pltpu.VMEM((width, width), BF)] * 6
        + [pltpu.VMEM((levels, width, width), BF)] * 2
        + [
            pltpu.VMEM((2, width, width), F32),
            pltpu.VMEM((steps * batch, width), F32),
            pltpu.VMEM((steps, batch, width), F32),
            pltpu.VMEM((steps, width), F32),
            pltpu.VMEM((steps, batch, width), F32),
            pltpu.VMEM((steps, batch, width), F32),
            pltpu.VMEM((steps // 2, batch, width), F32),
            pltpu.VMEM((steps // 4, batch, width), F32),
            pltpu.VMEM((2 * slabs, batch, width), F32),
            pltpu.SemaphoreType.DMA((3,)),
            pltpu.SemaphoreType.DMA,
        ]
        + [pltpu.SemaphoreType.DMA((slabs,))] * 4,
        compiler_params=pltpu.CompilerParams(
            vmem_limit_bytes=56 * 2**20, collective_id=0, has_side_effects=True
        ),
    )(
        readings, block_owner.reshape(1, -1), block_offset.reshape(1, -1), initial_mean,
        shrink_rate.reshape(1, -1), transition, input_map, smoother_gain,
    )


def solution(mesh):
    in_specs = (P("tm", "col", None), P("tm", None), P("tm"), P("col", None), P(), P(), P(), P())
    out_specs = (P("tm", "col", None), P("tm", "col", None))
    return jax.shard_map(
        per_device, mesh=mesh, in_specs=in_specs, out_specs=out_specs, check_vma=False
    )
```
